32 devices in a mesh: mom: 8 (over z, x), trow: 4 (over y, core).
Axes of the slice: x: 2, y: 2, z: 4, core: 2. Of those that a mesh axis runs over, the one named last changes fastest.
Arguments:
- lesser: bfloat16 [2, 256, 512, 512], P(None, 'mom', 'trow'), may hold values from -12 to 12
- greater: bfloat16 [2, 256, 512, 512], P(None, 'mom', 'trow'), may hold values from -12 to 12
- momentum_ids: int32 [256], replicated, may hold values from 0 to 255, each once
- window_start: int32 [1], replicated, may hold values from 0 to 2047
Outputs:
- collision: bfloat16 [2, 256, 512, 512], P(None, 'mom', 'trow')
The draws below stay inside these ranges and needn't reach their ends.
Inputs may be any that keep to these rules, and one draw needn't show every extreme that they name: Position j holds lattice momentum (momentum_ids[j] // 16, momentum_ids[j] % 16); every value appears once.
All inputs are finite; a program needn't handle non-finite values.
Results may differ from the reference program's by a relative error of at most 0.009.
Values may be sent and summed in bfloat16 or wider, within the bound.
No kernel may reach another device: no remote copies, remote signals or barrier semaphores. Data moves between devices by JAX's collectives and lax.ppermute only.
A program may use at most 192 MiB of HBM per device.

```python
import jax
import jax.numpy as jnp
from jax import lax

LX = 16
LY = 16
TW = 512
K = 256
DRIVE = 128


def shard_levels(own_key, dims, pieces, smallest, high):
    factor_of, own = 1.0, jax.random.fold_in(own_key, 6)
    for dim, shards_of in pieces:
        heights = jnp.exp(jax.random.uniform(jax.random.fold_in(own, dim), (shards_of,), jnp.float32, smallest / len(pieces), high / len(pieces)))
        factor_of = factor_of * jnp.repeat(heights, dims[dim] // shards_of).reshape([-1 if axis == dim else 1 for axis in range(len(dims))])
    return factor_of


def normal_values(key, shape, scale, most, pieces=(), kind=jnp.bfloat16):
    result = jax.random.normal(key, shape, jnp.float32) * scale
    if len(pieces) > 0:
        result = shard_levels(key, shape, pieces, -0.22, 0.18) * result
    return jnp.clip(result, min=-most, max=most).astype(kind)


def setup_inputs(seed: int = 0) -> dict:
    key_of = jax.random.split(jax.random.key(seed), 5)
    lesser = normal_values(key_of[0], (2, K, TW, TW), 2.0, 12.0, ((1, 8), (2, 4)))
    greater = normal_values(key_of[1], (2, K, TW, TW), 2.0, 12.0, ((1, 8), (2, 4)))
    momentum_ids = jax.random.permutation(key_of[2], K).astype(jnp.int32)
    window_start = jax.random.randint(key_of[3], (1,), 0, 4 * TW).astype(jnp.int32)
    return dict(lesser=lesser, greater=greater, momentum_ids=momentum_ids, window_start=window_start)


U_BASE = 4.0
TIME_STEP = 0.02


def lattice_tables(momentum_ids):
    momenta = momentum_ids.shape[0]
    wave_x = momentum_ids // LY
    wave_y = momentum_ids % LY
    sites = jnp.arange(momenta, dtype=jnp.int32)
    site_x = sites // LY
    site_y = sites % LY
    phase = ((wave_x[:, None] * site_x[None, :]) % LX) * LY + ((wave_y[:, None] * site_y[None, :]) % LY) * LX
    angle = (2.0 * jnp.pi / momenta) * (phase % momenta).astype(jnp.float32)
    return jnp.cos(angle), jnp.sin(angle), momenta


def transforms(momentum_ids):
    cos_table, sin_table, momenta = lattice_tables(momentum_ids)
    forward = jnp.stack([jnp.stack([cos_table, sin_table], 1), jnp.stack([-sin_table, cos_table], 1)], 0)
    forward = (forward / momenta).astype(jnp.bfloat16)
    backward = jnp.stack([jnp.stack([cos_table.T, -sin_table.T], 1), jnp.stack([sin_table.T, cos_table.T], 1)], 0)
    return forward, backward.astype(jnp.bfloat16)


def drive(window_start, row_times):
    phase = ((window_start[0] + row_times) % DRIVE).astype(jnp.float32)
    return U_BASE * (1.0 + 0.5 * jnp.sin((2.0 * jnp.pi / DRIVE) * phase))


def second_born(less_part, more_part, forward, backward, weight, retard_mask):
    table = forward.astype(jnp.float32)
    less_space = jnp.einsum('pkqc,pkor->orqc', less_part.astype(jnp.float32), table)
    more_space = jnp.einsum('pkqc,pkor->orqc', more_part.astype(jnp.float32), table)
    less_re, less_im = less_space[0], less_space[1]
    more_re, more_im = more_space[0], more_space[1]
    square_re = less_re * less_re - less_im * less_im
    square_im = 2.0 * less_re * less_im
    sigma_less_re = -weight * (square_re * more_re + square_im * more_im)
    sigma_less_im = -weight * (square_im * more_re - square_re * more_im)
    other_re = more_re * more_re - more_im * more_im
    other_im = 2.0 * more_re * more_im
    sigma_more_re = -weight * (other_re * less_re + other_im * less_im)
    sigma_more_im = -weight * (other_im * less_re - other_re * less_im)
    sigma_less_space = jnp.stack([sigma_less_re, sigma_less_im]).astype(jnp.bfloat16)
    sigma_more_space = jnp.stack([sigma_more_re, sigma_more_im]).astype(jnp.bfloat16)
    back_table = backward.astype(jnp.float32)
    less_mom = jnp.einsum('orqc,orsk->skqc', sigma_less_space.astype(jnp.float32), back_table)
    more_mom = jnp.einsum('orqc,orsk->skqc', sigma_more_space.astype(jnp.float32), back_table)
    sigma_ret = (retard_mask * (more_mom - less_mom)).astype(jnp.bfloat16)
    return sigma_ret, less_mom.astype(jnp.bfloat16)


def complex_dot(left_side, right_side):
    left_one = left_side.astype(jnp.float32)
    right_one = right_side.astype(jnp.float32)
    real_part = jnp.dot(left_one[0], right_one[0]) + jnp.dot(-left_one[1], right_one[1])
    imag_part = jnp.dot(left_one[0], right_one[1]) + jnp.dot(left_one[1], right_one[0])
    return jnp.stack([real_part, imag_part])


def reference(lesser, greater, momentum_ids, window_start):
    forward, backward = transforms(momentum_ids)
    row_block = 32
    block_count = TW // row_block
    col_index = jnp.arange(TW, dtype=jnp.int32)
    col_drive = drive(window_start, col_index)

    def rows_block(block_index):
        row_first = (block_index * row_block).astype(jnp.int32)
        less_part = lax.dynamic_slice_in_dim(lesser, row_first, row_block, 2)
        more_part = lax.dynamic_slice_in_dim(greater, row_first, row_block, 2)
        row_times = row_first + jnp.arange(row_block, dtype=jnp.int32)
        weight = drive(window_start, row_times)[:, None] * col_drive[None, :]
        retard_mask = (row_times[:, None] >= col_index[None, :]).astype(jnp.float32)
        return second_born(less_part, more_part, forward, backward, weight, retard_mask)

    ret_blocks, less_blocks = lax.map(rows_block, jnp.arange(block_count, dtype=jnp.int32))
    sigma_ret = jnp.transpose(ret_blocks, (1, 2, 0, 3, 4)).reshape(2, K, TW, TW)
    sigma_less = jnp.transpose(less_blocks, (1, 2, 0, 3, 4)).reshape(2, K, TW, TW)
    upper_mask = (col_index[:, None] <= col_index[None, :]).astype(jnp.float32)

    def per_momentum(items):
        ret_one, less_one, lower_fn, upper_fn = items
        advanced = (-upper_mask * (upper_fn.astype(jnp.float32) - lower_fn.astype(jnp.float32))).astype(jnp.bfloat16)
        return complex_dot(ret_one, lower_fn) + complex_dot(less_one, advanced)

    stacked = lax.map(per_momentum, (jnp.moveaxis(sigma_ret, 1, 0), jnp.moveaxis(sigma_less, 1, 0), jnp.moveaxis(lesser, 1, 0), jnp.moveaxis(greater, 1, 0)))
    summed = jnp.moveaxis(stacked, 0, 1)
    return (TIME_STEP * summed).astype(jnp.bfloat16)
```

```python
import functools

import jax
import jax.numpy as jnp
import numpy as np
from jax import lax
from jax.experimental import pallas as pl
from jax.experimental.pallas import tpu as pltpu
from jax.sharding import PartitionSpec as P

LX = 16
LY = 16
DRIVE = 128


U_BASE = 4.0
TIME_STEP = 0.02

COLUMN_PARTS = 2
VMEM_BYTES = 56 * 1024 * 1024


def lattice_tables(momentum_ids):
    momenta = momentum_ids.shape[0]
    wave_x = momentum_ids // LY
    wave_y = momentum_ids % LY
    sites = jnp.arange(momenta, dtype=jnp.int32)
    site_x = sites // LY
    site_y = sites % LY
    phase = (
        wave_x[:, None] * site_x[None, :] % LX * LY + wave_y[:, None] * site_y[None, :] % LY * LX
    )
    angle = 2.0 * jnp.pi / momenta * (phase % momenta).astype(jnp.float32)
    return (jnp.cos(angle), jnp.sin(angle), momenta)


def transforms(momentum_ids, groups):
    cos_table, sin_table, momenta = lattice_tables(momentum_ids)
    local_k = momenta // groups
    forward = jnp.stack(
        [jnp.stack([cos_table, sin_table], 1), jnp.stack([-sin_table, cos_table], 1)], 0
    )
    forward = (forward / momenta).astype(jnp.bfloat16)
    forward = forward.reshape(2, groups, local_k, 2, momenta).transpose(3, 4, 1, 0, 2)
    backward = jnp.stack(
        [jnp.stack([cos_table.T, -sin_table.T], 1), jnp.stack([sin_table.T, cos_table.T], 1)], 0
    ).astype(jnp.bfloat16)
    backward = backward.reshape(2, momenta, 2, groups, local_k).transpose(3, 2, 4, 0, 1)
    return (
        forward.reshape(2 * momenta, 2 * momenta),
        backward.reshape(2 * momenta, 2 * momenta),
    )


def drive(window_start, row_times):
    phase = ((window_start[0] + row_times) % DRIVE).astype(jnp.float32)
    return U_BASE * (1.0 + 0.5 * jnp.sin(2.0 * jnp.pi / DRIVE * phase))


def born_kernel(x_ref, forward_ref, backward_ref, weight_ref, mask_ref, out_ref):
    groups, _, _, depth, width = x_ref.shape
    half = groups * depth // 2
    table = forward_ref[...]
    weight = -weight_ref[0]
    less = jnp.dot(
        table, x_ref[:, 0, 0].reshape(groups * depth, width), preferred_element_type=jnp.float32
    )
    more = jnp.dot(
        table, x_ref[:, 1, 0].reshape(groups * depth, width), preferred_element_type=jnp.float32
    )
    less_re, less_im = (less[:half], less[half:])
    more_re, more_im = (more[:half], more[half:])
    square_re = less_re * less_re - less_im * less_im
    square_im = 2.0 * less_re * less_im
    sigma_less = jnp.concatenate(
        [
            (weight * (square_re * more_re + square_im * more_im)).astype(jnp.bfloat16),
            (weight * (square_im * more_re - square_re * more_im)).astype(jnp.bfloat16),
        ],
        axis=0,
    )
    other_re = more_re * more_re - more_im * more_im
    other_im = 2.0 * more_re * more_im
    sigma_more = jnp.concatenate(
        [
            (weight * (other_re * less_re + other_im * less_im)).astype(jnp.bfloat16),
            (weight * (other_im * less_re - other_re * less_im)).astype(jnp.bfloat16),
        ],
        axis=0,
    )
    back = backward_ref[...]
    less_mom = jnp.dot(back, sigma_less, preferred_element_type=jnp.float32)
    more_mom = jnp.dot(back, sigma_more, preferred_element_type=jnp.float32)
    ret = (mask_ref[0] * (more_mom - less_mom)).astype(jnp.bfloat16)
    out_ref[:, 0, 0] = less_mom.astype(jnp.bfloat16).reshape(groups, depth, width)
    out_ref[:, 1, 0] = ret.reshape(groups, depth, width)


def born(spread, forward, backward, weight, mask):
    groups, _, sub_rows, depth, width = spread.shape
    size = groups * depth
    return pl.pallas_call(
        born_kernel,
        grid=(sub_rows,),
        in_specs=[
            pl.BlockSpec((groups, 2, 1, depth, width), lambda i: (0, 0, i, 0, 0)),
            pl.BlockSpec((size, size), lambda i: (0, 0)),
            pl.BlockSpec((size, size), lambda i: (0, 0)),
            pl.BlockSpec((1, 1, width), lambda i: (i, 0, 0)),
            pl.BlockSpec((1, 1, width), lambda i: (i, 0, 0)),
        ],
        out_specs=pl.BlockSpec((groups, 2, 1, depth, width), lambda i: (0, 0, i, 0, 0)),
        out_shape=jax.ShapeDtypeStruct(spread.shape, jnp.bfloat16),
        compiler_params=pltpu.CompilerParams(vmem_limit_bytes=VMEM_BYTES),
        cost_estimate=pl.CostEstimate(
            flops=8 * size * size * sub_rows * width,
            bytes_accessed=4 * spread.size,
            transcendentals=0,
        ),
        name="born",
    )(spread, forward, backward, weight, mask)


def collide_kernel(first_col, last, sigma_ref, less_ref, more_ref, *refs):
    total_ref, out_ref = (None, refs[0]) if len(refs) == 1 else refs
    rows, cols = out_ref.shape[2:]
    steps = less_ref.shape[2]

    def left(kind, part):
        return sigma_ref[:, kind, part, 0].reshape(rows, steps)

    less_re, less_im = (less_ref[0, 0], less_ref[1, 0])
    step_index = first_col + lax.broadcasted_iota(jnp.int32, (steps, cols), 0)
    upper = step_index <= lax.broadcasted_iota(jnp.int32, (steps, cols), 1)

    def advanced(part):
        gap = less_ref[part, 0].astype(jnp.float32) - more_ref[part, 0].astype(jnp.float32)
        return jnp.where(upper, gap, 0.0).astype(jnp.bfloat16)

    right = jnp.concatenate([less_re, less_im, advanced(0), advanced(1)], axis=0)
    lesser_re, lesser_im = (left(0, 0), left(0, 1))
    ret_re, ret_im = (left(1, 0), left(1, 1))
    lefts = jnp.concatenate(
        [
            jnp.concatenate([ret_re, -ret_im, lesser_re, -lesser_im], axis=1),
            jnp.concatenate([ret_im, ret_re, lesser_im, lesser_re], axis=1),
        ],
        axis=0,
    )
    product = jnp.dot(lefts, right, preferred_element_type=jnp.float32)
    for part in range(2):
        value = product[part * rows : (part + 1) * rows]
        if total_ref is not None:
            value = total_ref[part, 0] + value
        if last:
            value = TIME_STEP * value
        out_ref[part, 0] = value.astype(out_ref.dtype)


def collide(sigma, less_all, more_all, total, first_col, last):
    groups, _, _, local_k, sub_rows, width = sigma.shape
    rows, cols = (groups * sub_rows, less_all.shape[3])
    sigma_spec = pl.BlockSpec(
        (groups, 2, 2, 1, sub_rows, width), lambda k: (0, 0, 0, k, 0, 0)
    )
    piece_spec = pl.BlockSpec((2, 1, width, cols), lambda k: (0, k, first_col // width, 0))
    out_spec = pl.BlockSpec((2, 1, rows, cols), lambda k: (0, k, 0, 0))
    totals = () if total is None else (total,)
    kind = jnp.bfloat16 if last else jnp.float32
    return pl.pallas_call(
        functools.partial(collide_kernel, first_col, last),
        grid=(local_k,),
        in_specs=[sigma_spec, piece_spec, piece_spec] + [out_spec] * len(totals),
        out_specs=out_spec,
        out_shape=jax.ShapeDtypeStruct((2, local_k, rows, cols), kind),
        compiler_params=pltpu.CompilerParams(vmem_limit_bytes=VMEM_BYTES),
        cost_estimate=pl.CostEstimate(
            flops=16 * local_k * rows * width * cols,
            bytes_accessed=2 * sigma.size + 8 * local_k * width * cols + 12 * local_k * rows * cols,
            transcendentals=0,
        ),
        name="collide",
    )(sigma, less_all, more_all, *totals)


def swap_groups(part):
    return lax.all_to_all(part, "mom", split_axis=0, concat_axis=0, tiled=True)


def on_device(lesser, greater, momentum_ids, window_start):
    _, local_k, row_count, col_count = lesser.shape
    groups = lax.axis_size("mom")
    sub_rows = row_count // groups
    width = col_count // COLUMN_PARTS
    row_first = lax.axis_index("trow") * row_count + lax.axis_index("mom") * sub_rows
    row_times = row_first + jnp.arange(sub_rows, dtype=jnp.int32)

    spreads = []
    for part in range(COLUMN_PARTS):
        both = jnp.stack([lesser, greater])[..., part * width : (part + 1) * width]
        both = both.reshape(2, 2, local_k, groups, sub_rows, width).transpose(3, 0, 4, 1, 2, 5)
        spreads.append(swap_groups(both.reshape(groups, 2, sub_rows, 2 * local_k, width)))

    less_all = lax.all_gather(lesser, "trow", axis=2, tiled=True)
    more_all = lax.all_gather(greater, "trow", axis=2, tiled=True)
    forward, backward = transforms(momentum_ids, groups)
    row_drive = drive(window_start, row_times)

    sigmas = []
    for part in range(COLUMN_PARTS):
        col_index = part * width + jnp.arange(width, dtype=jnp.int32)
        weight = row_drive[:, None] * drive(window_start, col_index)[None, :]
        mask = (row_times[:, None] >= col_index[None, :]).astype(jnp.float32)
        sigma = born(spreads[part], forward, backward, weight[:, None], mask[:, None])
        sigma = sigma.transpose(0, 1, 3, 2, 4)
        sigmas.append(swap_groups(sigma))

    total = None
    for part in range(COLUMN_PARTS):
        sigma = sigmas[part].reshape(groups, 2, 2, local_k, sub_rows, width)
        if sub_rows % 16:
            sigma = sigma.transpose(1, 2, 3, 0, 4, 5).reshape(
                1, 2, 2, local_k, groups * sub_rows, width
            )
        total = collide(
            sigma, less_all, more_all, total, part * width, part == COLUMN_PARTS - 1
        )
    return total


def solution(mesh):
    return jax.shard_map(
        on_device,
        mesh=mesh,
        in_specs=(P(None, "mom", "trow", None), P(None, "mom", "trow", None), P(), P()),
        out_specs=P(None, "mom", "trow", None),
        check_vma=False,
    )
```

```python
import functools

import jax
import jax.numpy as jnp
from jax import lax
from jax.experimental import pallas as pl
from jax.experimental.pallas import tpu as pltpu
from jax.sharding import PartitionSpec as P

LX = 16
LY = 16
DRIVE = 128


U_BASE = 4.0
TIME_STEP = 0.02

MOMENTA_BLOCK = 2
VMEM_BYTES = 56 * 1024 * 1024


def lattice_tables(momentum_ids):
    momenta = momentum_ids.shape[0]
    wave_x = momentum_ids // LY
    wave_y = momentum_ids % LY
    sites = jnp.arange(momenta, dtype=jnp.int32)
    site_x = sites // LY
    site_y = sites % LY
    phase = (
        wave_x[:, None] * site_x[None, :] % LX * LY + wave_y[:, None] * site_y[None, :] % LY * LX
    )
    angle = 2.0 * jnp.pi / momenta * (phase % momenta).astype(jnp.float32)
    return (jnp.cos(angle), jnp.sin(angle), momenta)


def transforms(momentum_ids, groups):
    cos_table, sin_table, momenta = lattice_tables(momentum_ids)
    local_k = momenta // groups
    forward = jnp.stack(
        [jnp.stack([cos_table, sin_table], 1), jnp.stack([-sin_table, cos_table], 1)], 0
    )
    forward = (forward / momenta).astype(jnp.bfloat16)
    forward = forward.reshape(2, groups, local_k, 2, momenta).transpose(3, 4, 1, 0, 2)
    backward = jnp.stack(
        [jnp.stack([cos_table.T, -sin_table.T], 1), jnp.stack([sin_table.T, cos_table.T], 1)], 0
    ).astype(jnp.bfloat16)
    backward = backward.reshape(2, momenta, 2, groups, local_k).transpose(3, 2, 4, 0, 1)
    return (
        forward.reshape(2 * momenta, 2 * momenta),
        backward.reshape(2 * momenta, 2 * momenta),
    )


def drive(window_start, row_times):
    phase = ((window_start[0] + row_times) % DRIVE).astype(jnp.float32)
    return U_BASE * (1.0 + 0.5 * jnp.sin(2.0 * jnp.pi / DRIVE * phase))


def born_kernel(pieces, *refs):
    x_refs = refs[:pieces]
    forward_ref, backward_ref, weight_ref, mask_ref, out_ref = refs[pieces:]
    half = forward_ref.shape[0] // 2
    table = forward_ref[...]
    weight = -weight_ref[0]
    less = jnp.dot(
        table,
        jnp.concatenate([ref[0, 0] for ref in x_refs], axis=0),
        preferred_element_type=jnp.float32,
    )
    more = jnp.dot(
        table,
        jnp.concatenate([ref[0, 1] for ref in x_refs], axis=0),
        preferred_element_type=jnp.float32,
    )
    less_re, less_im = (less[:half], less[half:])
    more_re, more_im = (more[:half], more[half:])
    square_re = less_re * less_re - less_im * less_im
    square_im = 2.0 * less_re * less_im
    sigma_less = jnp.concatenate(
        [
            (weight * (square_re * more_re + square_im * more_im)).astype(jnp.bfloat16),
            (weight * (square_im * more_re - square_re * more_im)).astype(jnp.bfloat16),
        ],
        axis=0,
    )
    other_re = more_re * more_re - more_im * more_im
    other_im = 2.0 * more_re * more_im
    sigma_more = jnp.concatenate(
        [
            (weight * (other_re * less_re + other_im * less_im)).astype(jnp.bfloat16),
            (weight * (other_im * less_re - other_re * less_im)).astype(jnp.bfloat16),
        ],
        axis=0,
    )
    back = backward_ref[...]
    less_mom = jnp.dot(back, sigma_less, preferred_element_type=jnp.float32)
    more_mom = jnp.dot(back, sigma_more, preferred_element_type=jnp.float32)
    ret = (mask_ref[0] * (more_mom - less_mom)).astype(jnp.bfloat16)
    _, _, _, depth, width = out_ref.shape
    out_ref[:, 0, 0] = less_mom.astype(jnp.bfloat16).reshape(pieces, depth, width)
    out_ref[:, 1, 0] = ret.reshape(pieces, depth, width)


def born(spread, forward, backward, weight, mask):
    pieces = len(spread)
    sub_rows, _, depth, width = spread[0].shape
    size = pieces * depth
    out_shape = (pieces, 2, sub_rows, depth, width)
    return pl.pallas_call(
        functools.partial(born_kernel, pieces),
        grid=(sub_rows,),
        in_specs=[pl.BlockSpec((1, 2, depth, width), lambda i: (i, 0, 0, 0))] * pieces
        + [
            pl.BlockSpec((size, size), lambda i: (0, 0)),
            pl.BlockSpec((size, size), lambda i: (0, 0)),
            pl.BlockSpec((1, 1, width), lambda i: (i, 0, 0)),
            pl.BlockSpec((1, 1, width), lambda i: (i, 0, 0)),
        ],
        out_specs=pl.BlockSpec((pieces, 2, 1, depth, width), lambda i: (0, 0, i, 0, 0)),
        out_shape=jax.ShapeDtypeStruct(out_shape, jnp.bfloat16),
        compiler_params=pltpu.CompilerParams(vmem_limit_bytes=VMEM_BYTES),
        cost_estimate=pl.CostEstimate(
            flops=8 * size * size * sub_rows * width,
            bytes_accessed=8 * size * sub_rows * width,
            transcendentals=0,
        ),
        name="born",
    )(*spread, forward, backward, weight, mask)


def sigma_rows(ref, part, index):
    pieces, _, _, sub_rows, width = ref.shape
    return ref[:, part, index].reshape(pieces * sub_rows, width)


def collide_kernel(plan, order_ref, *refs):
    n_ret, n_less, first_step, first_col, done_cols, has_total, has_lesser, has_rest = plan
    refs = list(refs)
    ret_refs = [refs.pop(0) for _ in range(n_ret)]
    less_refs = [refs.pop(0) for _ in range(n_less)]
    lesser_ref = refs.pop(0) if has_lesser else None
    gap_less_ref, gap_more_ref = (refs.pop(0), refs.pop(0))
    total_ref = refs.pop(0) if has_total else None
    if has_total:
        refs.pop(0)
    out_ref = refs.pop(0)
    rest_ref = refs.pop(0) if has_rest else None
    block, steps, cols = gap_less_ref.shape[1:]
    pieces, _, _, sub_rows, _ = less_refs[0].shape
    rows = pieces * sub_rows
    step_index = first_step + lax.broadcasted_iota(jnp.int32, (steps, cols), 0)
    upper = step_index <= first_col + lax.broadcasted_iota(jnp.int32, (steps, cols), 1)
    for index in range(block):

        def advanced(part):
            gap = gap_less_ref[part, index].astype(jnp.float32)
            gap = gap - gap_more_ref[part, index].astype(jnp.float32)
            return jnp.where(upper, gap, 0.0).astype(jnp.bfloat16)

        re = [sigma_rows(ref, 0, index) for ref in less_refs]
        im = [sigma_rows(ref, 1, index) for ref in less_refs]
        top, low = (re + [-v for v in im], im + re)
        right = [advanced(0), advanced(1)]
        if has_lesser:
            re = [sigma_rows(ref, 0, index) for ref in ret_refs]
            im = [sigma_rows(ref, 1, index) for ref in ret_refs]
            top, low = (top + re + [-v for v in im], low + im + re)
            right = right + [lesser_ref[0, index], lesser_ref[1, index]]
        left = jnp.concatenate(
            [jnp.concatenate(top, axis=1), jnp.concatenate(low, axis=1)], axis=0
        )
        product = jnp.dot(
            left, jnp.concatenate(right, axis=0), preferred_element_type=jnp.float32
        )
        for part in range(2):
            value = product[part * rows : (part + 1) * rows]
            if has_total:
                value = total_ref[part, index] + value
            done = (TIME_STEP * value[:, :done_cols]).astype(out_ref.dtype)
            for piece in range(pieces):
                first = pl.multiple_of(order_ref[piece] * sub_rows, sub_rows)
                out_ref[part, index, pl.ds(first, sub_rows), :] = done[
                    piece * sub_rows : (piece + 1) * sub_rows
                ]
            if has_rest:
                rest_ref[part, index] = value[:, done_cols:]


def collide(order, rets, lesses, less_all, more_all, carried, first_step, first_col, done_cols):
    pieces, _, local_k, sub_rows, _ = lesses[0].shape
    col_count = less_all.shape[3]
    rows, steps, cols = (pieces * sub_rows, sum(s.shape[4] for s in lesses), col_count - first_col)
    block = min(MOMENTA_BLOCK, local_k)
    has_rest = done_cols < cols

    def sigma_spec(array):
        shape = (pieces, 2, block, sub_rows, array.shape[4])
        return pl.BlockSpec(shape, lambda k, order: (0, 0, k, 0, 0))

    arrays, specs = ([*rets, *lesses], [sigma_spec(a) for a in (*rets, *lesses)])
    if rets:
        arrays.append(less_all)
        specs.append(
            pl.BlockSpec((2, block, col_count, cols), lambda k, order: (0, k, 0, first_col // cols))
        )
    gap_index = (first_step // steps, first_col // cols)
    gap_spec = pl.BlockSpec((2, block, steps, cols), lambda k, order: (0, k, *gap_index))
    arrays += [less_all, more_all]
    specs += [gap_spec, gap_spec]
    aliases = {}
    if carried is not None:
        arrays += list(carried)
        specs += [
            pl.BlockSpec((2, block, rows, cols), lambda k, order: (0, k, 0, 0)),
            pl.BlockSpec(memory_space=pl.ANY),
        ]
        aliases = {len(arrays): 0}
    out_specs = [
        pl.BlockSpec((2, block, rows, done_cols), lambda k, order: (0, k, 0, first_col // done_cols))
    ]
    out_shape = [jax.ShapeDtypeStruct((2, local_k, rows, col_count), jnp.bfloat16)]
    if has_rest:
        rest = cols - done_cols
        out_specs.append(pl.BlockSpec((2, block, rows, rest), lambda k, order: (0, k, 0, 0)))
        out_shape.append(jax.ShapeDtypeStruct((2, local_k, rows, rest), jnp.float32))
    plan = (
        len(rets),
        len(lesses),
        first_step,
        first_col,
        done_cols,
        carried is not None,
        bool(rets),
        has_rest,
    )
    depth = steps + (col_count if rets else 0)
    results = pl.pallas_call(
        functools.partial(collide_kernel, plan),
        grid_spec=pltpu.PrefetchScalarGridSpec(
            num_scalar_prefetch=1, grid=(local_k // block,), in_specs=specs, out_specs=out_specs
        ),
        out_shape=out_shape,
        input_output_aliases=aliases,
        compiler_params=pltpu.CompilerParams(vmem_limit_bytes=VMEM_BYTES),
        cost_estimate=pl.CostEstimate(
            flops=8 * local_k * rows * depth * cols,
            bytes_accessed=4 * local_k * (depth + steps) * (cols + rows)
            + 12 * local_k * rows * cols,
            transcendentals=0,
        ),
        name="collide",
    )(order, *arrays)
    return (results[1] if has_rest else None, results[0])


def on_device(lesser, greater, momentum_ids, window_start):
    _, local_k, row_count, col_count = lesser.shape
    groups, ranks = (lax.axis_size("mom"), lax.axis_size("trow"))
    group = lax.axis_index("mom")
    sub_rows = row_count // groups
    order = group ^ jnp.arange(groups, dtype=jnp.int32)
    far, near = (list(range(groups // 2, groups)), list(range(1, groups // 2)))
    offsets = [d for pair in zip(far, near + [0]) for d in pair if d]

    def send(array, offset, first_rank=0):
        pairs = [
            (g * ranks + r, (g ^ offset) * ranks + r)
            for g in range(groups)
            for r in range(first_rank, ranks)
        ]
        return lax.ppermute(array, ("mom", "trow"), pairs)

    row_first = lax.axis_index("trow") * row_count + group * sub_rows
    row_times = row_first + jnp.arange(sub_rows, dtype=jnp.int32)
    width = col_count // 4

    def pack(offset, first, count):
        def rows_of(array):
            return lax.dynamic_slice(
                array,
                (0, 0, (group ^ offset) * sub_rows, first),
                (2, local_k, sub_rows, count),
            )

        both = jnp.stack([rows_of(lesser), rows_of(greater)])
        both = both.transpose(3, 0, 1, 2, 4)
        return both.reshape(sub_rows, 2, 2 * local_k, count)

    halves = [(0, 2 * width), (2 * width, 2 * width)]
    spreads = []
    for first, count in halves:
        spread = {0: pack(0, first, count)}
        for d in offsets:
            spread[d] = send(pack(d, first, count), d)
        spreads.append([spread[d] for d in range(groups)])

    less_all = lax.all_gather(lesser, "trow", axis=2, tiled=True)
    more_all = lax.all_gather(greater, "trow", axis=2, tiled=True)
    forward, backward = transforms(
        momentum_ids.reshape(groups, local_k)[order].reshape(-1), groups
    )
    row_drive = drive(window_start, row_times)

    def born_part(part):
        first, count = halves[part]
        col_index = first + jnp.arange(count, dtype=jnp.int32)
        weight = row_drive[:, None] * drive(window_start, col_index)[None, :]
        mask = (row_times[:, None] >= col_index[None, :]).astype(jnp.float32)
        return born(spreads[part], forward, backward, weight[:, None], mask[:, None])

    def exchange(sigma, kind, first, count, col_first):
        first_rank = 0 if kind == 0 else min(r for r in range(ranks) if (r + 1) * row_count > col_first)
        got = {}
        for d in [*offsets, 0]:
            piece = sigma[d, kind, :, :, first : first + count].transpose(1, 0, 2)
            got[d] = send(piece, d, first_rank) if d else piece
        pieces = jnp.stack([got[d] for d in range(groups)])
        pieces = pieces.reshape(groups, 2, local_k, sub_rows, count)
        if sub_rows % 16 == 0:
            return pieces
        pieces = pieces[order].transpose(1, 2, 0, 3, 4)
        return pieces.reshape(1, 2, local_k, groups * sub_rows, count)

    sigma = born_part(0)
    ret_low = exchange(sigma, 1, 0, 2 * width, 0)
    less_low = exchange(sigma, 0, 0, 2 * width, 0)
    sigma = born_part(1)
    ret_mid = exchange(sigma, 1, 0, width, 2 * width)
    ret_high = exchange(sigma, 1, width, width, 3 * width)
    less_mid = exchange(sigma, 0, 0, width, 2 * width)
    less_high = exchange(sigma, 0, width, width, 3 * width)
    if sub_rows % 16:
        order = jnp.zeros((1,), jnp.int32)
    carried = collide(
        order, [ret_low, ret_mid, ret_high], [less_low], less_all, more_all, None, 0, 0, 2 * width
    )
    carried = collide(
        order, [], [less_mid], less_all, more_all, carried, 2 * width, 2 * width, width
    )
    carried = collide(
        order, [], [less_high], less_all, more_all, carried, 3 * width, 3 * width, width
    )
    return carried[1]


def solution(mesh):
    return jax.shard_map(
        on_device,
        mesh=mesh,
        in_specs=(P(None, "mom", "trow", None), P(None, "mom", "trow", None), P(), P()),
        out_specs=P(None, "mom", "trow", None),
        check_vma=False,
    )
```

```python
import functools

import jax
import jax.numpy as jnp
from jax import lax
from jax.experimental import pallas as pl
from jax.experimental.layout import Layout, with_layout_constraint
from jax.experimental.pallas import tpu as pltpu
from jax.sharding import PartitionSpec as P

LX = 16
LY = 16
DRIVE = 128


U_BASE = 4.0
TIME_STEP = 0.02

FAR_WINDOW = 2
NEAR_WINDOW = 2
VMEM_BYTES = 56 * 1024 * 1024


def lattice_tables(momentum_ids):
    momenta = momentum_ids.shape[0]
    wave_x = momentum_ids // LY
    wave_y = momentum_ids % LY
    sites = jnp.arange(momenta, dtype=jnp.int32)
    site_x = sites // LY
    site_y = sites % LY
    phase = (
        wave_x[:, None] * site_x[None, :] % LX * LY + wave_y[:, None] * site_y[None, :] % LY * LX
    )
    angle = 2.0 * jnp.pi / momenta * (phase % momenta).astype(jnp.float32)
    return (jnp.cos(angle), jnp.sin(angle), momenta)


def transforms(momentum_ids, groups):
    cos_table, sin_table, momenta = lattice_tables(momentum_ids)
    local_k = momenta // groups
    forward = jnp.stack(
        [jnp.stack([cos_table, sin_table], 1), jnp.stack([-sin_table, cos_table], 1)], 0
    )
    forward = (forward / momenta).astype(jnp.bfloat16)
    forward = forward.reshape(2, groups, local_k, 2, momenta).transpose(3, 4, 1, 0, 2)
    backward = jnp.stack(
        [jnp.stack([cos_table.T, -sin_table.T], 1), jnp.stack([sin_table.T, cos_table.T], 1)], 0
    ).astype(jnp.bfloat16)
    backward = backward.reshape(2, momenta, 2, groups, local_k).transpose(3, 2, 4, 0, 1)
    return (
        forward.reshape(2 * momenta, 2 * momenta),
        backward.reshape(2 * momenta, 2 * momenta),
    )


def drive(window_start, row_times):
    phase = ((window_start[0] + row_times) % DRIVE).astype(jnp.float32)
    return U_BASE * (1.0 + 0.5 * jnp.sin(2.0 * jnp.pi / DRIVE * phase))


def born_kernel(pieces, order_ref, *refs):
    x_refs = refs[:pieces]
    forward_ref, backward_ref, weight_ref, mask_ref, out_ref = refs[pieces:]
    half = forward_ref.shape[0] // 2
    table = forward_ref[...]
    weight = -weight_ref[0]
    less = jnp.dot(
        table,
        jnp.concatenate([ref[0, 0] for ref in x_refs], axis=0),
        preferred_element_type=jnp.float32,
    )
    more = jnp.dot(
        table,
        jnp.concatenate([ref[0, 1] for ref in x_refs], axis=0),
        preferred_element_type=jnp.float32,
    )
    less_re, less_im = (less[:half], less[half:])
    more_re, more_im = (more[:half], more[half:])
    square_re = less_re * less_re - less_im * less_im
    square_im = 2.0 * less_re * less_im
    sigma_less = jnp.concatenate(
        [
            (weight * (square_re * more_re + square_im * more_im)).astype(jnp.bfloat16),
            (weight * (square_im * more_re - square_re * more_im)).astype(jnp.bfloat16),
        ],
        axis=0,
    )
    other_re = more_re * more_re - more_im * more_im
    other_im = 2.0 * more_re * more_im
    sigma_more = jnp.concatenate(
        [
            (weight * (other_re * less_re + other_im * less_im)).astype(jnp.bfloat16),
            (weight * (other_im * less_re - other_re * less_im)).astype(jnp.bfloat16),
        ],
        axis=0,
    )
    back = backward_ref[...]
    less_mom = jnp.dot(back, sigma_less, preferred_element_type=jnp.float32)
    more_mom = jnp.dot(back, sigma_more, preferred_element_type=jnp.float32)
    ret = (mask_ref[0] * (more_mom - less_mom)).astype(jnp.bfloat16)
    _, _, _, depth, width = out_ref.shape
    kinds = (less_mom.astype(jnp.bfloat16), ret)
    for piece in range(pieces):
        for kind in range(2):
            rows = kinds[kind][piece * depth : (piece + 1) * depth]
            out_ref[order_ref[piece], kind, 0] = rows


def born(order, spread, forward, backward, weight, mask):
    pieces = len(spread)
    sub_rows, _, depth, width = spread[0].shape
    size = pieces * depth
    out_shape = (pieces, 2, sub_rows, depth, width)
    grid_spec = pltpu.PrefetchScalarGridSpec(
        num_scalar_prefetch=1,
        grid=(sub_rows,),
        in_specs=[pl.BlockSpec((1, 2, depth, width), lambda i, order: (i, 0, 0, 0))] * pieces
        + [
            pl.BlockSpec((size, size), lambda i, order: (0, 0)),
            pl.BlockSpec((size, size), lambda i, order: (0, 0)),
            pl.BlockSpec((1, 1, width), lambda i, order: (i, 0, 0)),
            pl.BlockSpec((1, 1, width), lambda i, order: (i, 0, 0)),
        ],
        out_specs=pl.BlockSpec(
            (pieces, 2, 1, depth, width), lambda i, order: (0, 0, i, 0, 0)
        ),
    )
    return pl.pallas_call(
        functools.partial(born_kernel, pieces),
        grid_spec=grid_spec,
        out_shape=jax.ShapeDtypeStruct(out_shape, jnp.bfloat16),
        compiler_params=pltpu.CompilerParams(vmem_limit_bytes=VMEM_BYTES),
        cost_estimate=pl.CostEstimate(
            flops=8 * size * size * sub_rows * width,
            bytes_accessed=8 * size * sub_rows * width,
            transcendentals=0,
        ),
        name="born",
    )(order, *spread, forward, backward, weight, mask)


def sigma_rows(ref, kind, part, index, order_ref):
    if order_ref is None:
        value = ref[:, kind, part, index]
    else:
        places = range(ref.shape[0])
        value = jnp.stack([ref[order_ref[place], kind, part, index] for place in places])
    return value.reshape(value.shape[0] * value.shape[1], value.shape[2])


def complex_left(terms, index, order_ref):
    re = [sigma_rows(ref, kind, 0, index, order_ref) for ref, kind in terms]
    im = [sigma_rows(ref, kind, 1, index, order_ref) for ref, kind in terms]
    top, low = (re + [-v for v in im], im + re)
    return jnp.concatenate(
        [jnp.concatenate(top, axis=1), jnp.concatenate(low, axis=1)], axis=0
    )


def collide_kernel(plan, order_ref, *refs):
    count, ret_terms, less_terms, first_col, gap_step, gap_col, has_total, has_old, has_rest, mixed = plan
    order_ref = order_ref if mixed else None
    refs = list(refs)
    sources = [refs.pop(0) for _ in range(count)]
    lesser_ref = refs.pop(0) if ret_terms else None
    gap_less_ref, gap_more_ref = (refs.pop(0), refs.pop(0))
    total_ref = refs.pop(0) if has_total else None
    if has_old:
        refs.pop(0)
    out_ref = refs.pop(0) if not has_rest or len(refs) == 2 else None
    rest_ref = refs.pop(0) if has_rest else None
    block, steps, gap_cols = gap_less_ref.shape[1:]
    rows = sources[0].shape[0] * sources[0].shape[4]
    done_cols = out_ref.shape[3] if out_ref is not None else 0
    shape = (steps, gap_cols)
    step_index = gap_step + lax.broadcasted_iota(jnp.int32, shape, 0)
    upper = step_index <= gap_col + lax.broadcasted_iota(jnp.int32, shape, 1)
    ret_terms = [(sources[source], kind) for source, kind in ret_terms]
    less_terms = [(sources[source], kind) for source, kind in less_terms]
    for index in range(block):

        def advanced(part):
            gap = gap_less_ref[part, index].astype(jnp.float32)
            gap = gap - gap_more_ref[part, index].astype(jnp.float32)
            return jnp.where(upper, gap, 0.0).astype(jnp.bfloat16)

        def product(left, *right):
            return jnp.dot(
                left, jnp.concatenate(right, axis=0), preferred_element_type=jnp.float32
            )

        left = complex_left(less_terms, index, order_ref)
        if not ret_terms:
            value = product(left, advanced(0), advanced(1))
        elif gap_col == first_col:
            value = product(
                jnp.concatenate([left, complex_left(ret_terms, index, order_ref)], axis=1),
                advanced(0),
                advanced(1),
                lesser_ref[0, index],
                lesser_ref[1, index],
            )
        else:
            value = product(
                complex_left(ret_terms, index, order_ref), lesser_ref[0, index], lesser_ref[1, index]
            )
            skipped = gap_col - first_col
            value = jnp.concatenate(
                [
                    value[:, :skipped],
                    value[:, skipped:] + product(left, advanced(0), advanced(1)),
                ],
                axis=1,
            )
        for part in range(2):
            one = value[part * rows : (part + 1) * rows]
            if has_total:
                one = total_ref[part, index] + one
            if out_ref is not None:
                out_ref[part, index] = (TIME_STEP * one[:, :done_cols]).astype(out_ref.dtype)
            if rest_ref is not None:
                rest_ref[part, index] = one[:, done_cols:]


def collide(order, sources, ret, less, functions, carried, cols, block, mixed=False):
    ret_terms, ret_step, ret_steps = ret
    less_terms, gap_step, gap_steps, gap_col = less
    less_all, more_all = functions
    first_col, last_col = cols
    total, output = carried
    _, local_k, _, col_count = less_all.shape
    rows = sources[0].shape[0] * sources[0].shape[4]
    span = col_count - first_col
    block = min(block, local_k)
    done_cols = last_col - first_col
    arrays, specs = ([], [])

    def take(array, shape, *place):
        arrays.append(array)
        specs.append(pl.BlockSpec(shape, lambda k, order: (0, k, *place)))

    for array in sources:
        count, kinds, _, _, sub_rows, width = array.shape
        arrays.append(array)
        specs.append(
            pl.BlockSpec(
                (count, kinds, 2, block, sub_rows, width), lambda k, order: (0, 0, 0, k, 0, 0)
            )
        )
    if ret_terms:
        take(less_all, (2, block, ret_steps, span), ret_step // ret_steps, first_col // span)
    gap_span = col_count - gap_col
    for array in (less_all, more_all):
        take(array, (2, block, gap_steps, gap_span), gap_step // gap_steps, gap_col // gap_span)
    if total is not None:
        take(total, (2, block, rows, span), 0, 0)
    out_specs, out_shape, aliases = ([], [], {})
    if done_cols:
        if output is not None:
            arrays.append(output)
            specs.append(pl.BlockSpec(memory_space=pl.ANY))
            aliases = {len(arrays): 0}
        out_specs.append(
            pl.BlockSpec(
                (2, block, rows, done_cols), lambda k, order: (0, k, 0, first_col // done_cols)
            )
        )
        out_shape.append(jax.ShapeDtypeStruct((2, local_k, rows, col_count), jnp.bfloat16))
    has_rest = last_col < col_count
    if has_rest:
        rest = col_count - last_col
        out_specs.append(pl.BlockSpec((2, block, rows, rest), lambda k, order: (0, k, 0, 0)))
        out_shape.append(jax.ShapeDtypeStruct((2, local_k, rows, rest), jnp.float32))
    plan = (
        len(sources),
        ret_terms,
        less_terms,
        first_col,
        gap_step,
        gap_col,
        total is not None,
        bool(aliases),
        has_rest,
        mixed,
    )
    work = ret_steps * span + gap_steps * gap_span
    results = list(
        pl.pallas_call(
            functools.partial(collide_kernel, plan),
            grid_spec=pltpu.PrefetchScalarGridSpec(
                num_scalar_prefetch=1, grid=(local_k // block,), in_specs=specs, out_specs=out_specs
            ),
            out_shape=out_shape,
            input_output_aliases=aliases,
            compiler_params=pltpu.CompilerParams(vmem_limit_bytes=VMEM_BYTES),
            cost_estimate=pl.CostEstimate(
                flops=8 * local_k * rows * work,
                bytes_accessed=12 * local_k * work + 8 * local_k * rows * span,
                transcendentals=0,
            ),
            name="collide",
        )(order, *arrays)
    )
    output = results.pop(0) if done_cols else None
    return (results.pop(0) if has_rest else None, output)


def on_device(lesser, greater, momentum_ids, window_start):
    _, local_k, row_count, col_count = lesser.shape
    groups, ranks = (lax.axis_size("mom"), lax.axis_size("trow"))
    group = lax.axis_index("mom")
    sub_rows = row_count // groups
    depth = 2 * local_k
    order = group ^ jnp.arange(groups, dtype=jnp.int32)
    far, near = (list(range(groups // 2, groups)), list(range(1, groups // 2)))
    offsets = [d for pair in zip(far, near + [0]) for d in pair if d]
    arrived = {True: [], False: []}

    def send(make, arrays, offset):
        is_far = 2 * offset >= groups
        queue, ahead = (arrived[is_far], FAR_WINDOW if is_far else NEAR_WINDOW)
        if len(queue) >= ahead:
            arrays, _ = lax.optimization_barrier((arrays, queue[-ahead]))
        pairs = [(g * ranks + r, (g ^ offset) * ranks + r) for g in range(groups) for r in range(ranks)]
        queue.append(lax.ppermute(make(*arrays), ("mom", "trow"), pairs))
        return queue[-1]

    def pack(offset, first, count, arrays):
        def rows_of(array):
            return lax.dynamic_slice(
                array,
                (0, 0, (group ^ offset) * sub_rows, first),
                (2, local_k, sub_rows, count),
            )

        both = jnp.stack([rows_of(array) for array in arrays])
        return both.transpose(3, 0, 1, 2, 4).reshape(sub_rows, 2, depth, count)

    width = col_count // 4
    halves = [(0, 3 * width), (3 * width, width)]
    row_first = lax.axis_index("trow") * row_count + group * sub_rows
    row_times = row_first + jnp.arange(sub_rows, dtype=jnp.int32)
    spreads = []
    for first, count in halves:
        spread = {0: pack(0, first, count, (lesser, greater))}
        for d in offsets:
            spread[d] = send(
                lambda *arrays: pack(d, first, count, arrays), (lesser, greater), d
            )
        spreads.append([spread[d] for d in range(groups)])

    functions = tuple(
        lax.all_gather(array, "trow", axis=2, tiled=True) for array in (lesser, greater)
    )
    forward, backward = transforms(
        momentum_ids.reshape(groups, local_k)[order].reshape(-1), groups
    )
    row_drive = drive(window_start, row_times)

    def born_part(part, before=None):
        first, count = halves[part]
        col_index = first + jnp.arange(count, dtype=jnp.int32)
        weight = row_drive[:, None] * drive(window_start, col_index)[None, :]
        mask = (row_times[:, None] >= col_index[None, :]).astype(jnp.float32)
        if before is not None:
            weight, _ = lax.optimization_barrier((weight, before))
        sigma = born(order, spreads[part], forward, backward, weight[:, None], mask[:, None])
        return with_layout_constraint(sigma.transpose(0, 1, 3, 2, 4), Layout((0, 1, 2, 3, 4)))

    def exchange(make, sigma, before=None, before_last=None):
        got = {}
        for d in offsets:
            after = before_last if d == far[-1] and before_last is not None else before
            held = sigma
            if after is not None:
                held, _ = lax.optimization_barrier((sigma, after))
            got[d] = send(lambda array: make(array[group ^ d]), (held,), d)
        got[0] = make(sigma[group])
        got = jnp.stack([got[d] for d in range(groups)])
        kinds, count = (got.shape[1], got.shape[4])
        got = got.reshape(groups, kinds, 2, local_k, sub_rows, count)
        if sub_rows % 16 == 0:
            return got
        got = got[order].transpose(1, 2, 3, 0, 4, 5)
        return got.reshape(1, kinds, 2, local_k, groups * sub_rows, count)

    mixed = sub_rows % 16 == 0
    sigma = born_part(0)
    low = exchange(lambda array: array, sigma)
    low_total, _ = collide(
        order,
        [low],
        ([(0, 1)], 0, 3 * width),
        ([(0, 0)], 0, 3 * width, 0),
        functions,
        (None, None),
        (0, 0),
        2,
        mixed,
    )
    sigma = born_part(1)
    high = exchange(lambda array: array, sigma, None, low_total)
    _, output = collide(
        order,
        [high],
        ([(0, 1)], 3 * width, width),
        ([(0, 0)], 3 * width, width, 3 * width),
        functions,
        (low_total, None),
        (0, col_count),
        4,
        mixed,
    )
    return output


def solution(mesh):
    return jax.shard_map(
        on_device,
        mesh=mesh,
        in_specs=(P(None, "mom", "trow", None), P(None, "mom", "trow", None), P(), P()),
        out_specs=P(None, "mom", "trow", None),
        check_vma=False,
    )
```

```python
import functools

import jax
import jax.numpy as jnp
from jax import lax
from jax.experimental import pallas as pl
from jax.experimental.layout import Layout, with_layout_constraint
from jax.experimental.pallas import tpu as pltpu
from jax.sharding import PartitionSpec as P

LX = 16
LY = 16
DRIVE = 128


U_BASE = 4.0
TIME_STEP = 0.02

FAR_WINDOW = 2
NEAR_WINDOW = 2
LATE_WINDOW = 5
VMEM_BYTES = 56 * 1024 * 1024


def lattice_tables(momentum_ids):
    momenta = momentum_ids.shape[0]
    wave_x = momentum_ids // LY
    wave_y = momentum_ids % LY
    sites = jnp.arange(momenta, dtype=jnp.int32)
    site_x = sites // LY
    site_y = sites % LY
    phase = (
        wave_x[:, None] * site_x[None, :] % LX * LY + wave_y[:, None] * site_y[None, :] % LY * LX
    )
    angle = 2.0 * jnp.pi / momenta * (phase % momenta).astype(jnp.float32)
    return (jnp.cos(angle), jnp.sin(angle), momenta)


def transforms(momentum_ids, groups):
    cos_table, sin_table, momenta = lattice_tables(momentum_ids)
    local_k = momenta // groups
    forward = jnp.stack(
        [jnp.stack([cos_table, sin_table], 1), jnp.stack([-sin_table, cos_table], 1)], 0
    )
    forward = (forward / momenta).astype(jnp.bfloat16)
    forward = forward.reshape(2, groups, local_k, 2, momenta).transpose(3, 4, 1, 0, 2)
    backward = jnp.stack(
        [jnp.stack([cos_table.T, -sin_table.T], 1), jnp.stack([sin_table.T, cos_table.T], 1)], 0
    ).astype(jnp.bfloat16)
    backward = backward.reshape(2, momenta, 2, groups, local_k).transpose(3, 2, 4, 0, 1)
    return (
        forward.reshape(2 * momenta, 2 * momenta),
        backward.reshape(2 * momenta, 2 * momenta),
    )


def drive(window_start, row_times):
    phase = ((window_start[0] + row_times) % DRIVE).astype(jnp.float32)
    return U_BASE * (1.0 + 0.5 * jnp.sin(2.0 * jnp.pi / DRIVE * phase))


def born_kernel(pieces, order_ref, *refs):
    x_refs = refs[:pieces]
    forward_ref, backward_ref, weight_ref, mask_ref, out_ref = refs[pieces:]
    half = forward_ref.shape[0] // 2
    table = forward_ref[...]
    weight = -weight_ref[0]
    less = jnp.dot(
        table,
        jnp.concatenate([ref[0, 0, 0] for ref in x_refs], axis=0),
        preferred_element_type=jnp.float32,
    )
    more = jnp.dot(
        table,
        jnp.concatenate([ref[0, 0, 1] for ref in x_refs], axis=0),
        preferred_element_type=jnp.float32,
    )
    less_re, less_im = (less[:half], less[half:])
    more_re, more_im = (more[:half], more[half:])
    square_re = less_re * less_re - less_im * less_im
    square_im = 2.0 * less_re * less_im
    sigma_less = jnp.concatenate(
        [
            (weight * (square_re * more_re + square_im * more_im)).astype(jnp.bfloat16),
            (weight * (square_im * more_re - square_re * more_im)).astype(jnp.bfloat16),
        ],
        axis=0,
    )
    other_re = more_re * more_re - more_im * more_im
    other_im = 2.0 * more_re * more_im
    sigma_more = jnp.concatenate(
        [
            (weight * (other_re * less_re + other_im * less_im)).astype(jnp.bfloat16),
            (weight * (other_im * less_re - other_re * less_im)).astype(jnp.bfloat16),
        ],
        axis=0,
    )
    back = backward_ref[...]
    less_mom = jnp.dot(back, sigma_less, preferred_element_type=jnp.float32)
    more_mom = jnp.dot(back, sigma_more, preferred_element_type=jnp.float32)
    ret = (mask_ref[0] * (more_mom - less_mom)).astype(jnp.bfloat16)
    _, _, _, depth, width = out_ref.shape
    kinds = (less_mom.astype(jnp.bfloat16), ret)
    for piece in range(pieces):
        for kind in range(2):
            rows = kinds[kind][piece * depth : (piece + 1) * depth]
            out_ref[order_ref[piece], kind, 0] = rows


def born(order, spread, forward, backward, weight, mask):
    if isinstance(spread, list):
        places = [lambda i, order: (0, i, 0, 0, 0)] * len(spread)
    else:
        places = [
            lambda i, order, place=place: (order[place], i, 0, 0, 0)
            for place in range(spread.shape[0])
        ]
        spread = [spread] * len(places)
    pieces = len(spread)
    _, sub_rows, _, depth, width = spread[0].shape
    size = pieces * depth
    out_shape = (pieces, 2, sub_rows, depth, width)
    grid_spec = pltpu.PrefetchScalarGridSpec(
        num_scalar_prefetch=1,
        grid=(sub_rows,),
        in_specs=[pl.BlockSpec((1, 1, 2, depth, width), place) for place in places]
        + [
            pl.BlockSpec((size, size), lambda i, order: (0, 0)),
            pl.BlockSpec((size, size), lambda i, order: (0, 0)),
            pl.BlockSpec((1, 1, width), lambda i, order: (i, 0, 0)),
            pl.BlockSpec((1, 1, width), lambda i, order: (i, 0, 0)),
        ],
        out_specs=pl.BlockSpec(
            (pieces, 2, 1, depth, width), lambda i, order: (0, 0, i, 0, 0)
        ),
    )
    return pl.pallas_call(
        functools.partial(born_kernel, pieces),
        grid_spec=grid_spec,
        out_shape=jax.ShapeDtypeStruct(out_shape, jnp.bfloat16),
        compiler_params=pltpu.CompilerParams(vmem_limit_bytes=VMEM_BYTES),
        cost_estimate=pl.CostEstimate(
            flops=8 * size * size * sub_rows * width,
            bytes_accessed=8 * size * sub_rows * width,
            transcendentals=0,
        ),
        name="born",
    )(order, *spread, forward, backward, weight, mask)


def sigma_rows(ref, kind, part, index, order_ref):
    if order_ref is None:
        value = ref[:, kind, part, index]
    else:
        places = range(ref.shape[0])
        value = jnp.stack([ref[order_ref[place], kind, part, index] for place in places])
    return value.reshape(value.shape[0] * value.shape[1], value.shape[2])


def complex_left(terms, index):
    re = [sigma_rows(ref, kind, 0, index, order_ref) for ref, order_ref, kind in terms]
    im = [sigma_rows(ref, kind, 1, index, order_ref) for ref, order_ref, kind in terms]
    top, low = (re + [-v for v in im], im + re)
    return jnp.concatenate(
        [jnp.concatenate(top, axis=1), jnp.concatenate(low, axis=1)], axis=0
    )


def collide_kernel(plan, order_ref, *refs):
    count, ret_terms, less_terms, first_col, gap_step, gap_col, has_total, has_old, has_rest, mixed = plan
    refs = list(refs)
    sources = [(refs.pop(0), order_ref if place in mixed else None) for place in range(count)]
    lesser_ref = refs.pop(0) if ret_terms else None
    gap_less_ref, gap_more_ref = (refs.pop(0), refs.pop(0))
    total_ref = refs.pop(0) if has_total else None
    if has_old:
        refs.pop(0)
    out_ref = refs.pop(0) if not has_rest or len(refs) == 2 else None
    rest_ref = refs.pop(0) if has_rest else None
    block, steps, gap_cols = gap_less_ref.shape[1:]
    rows = sources[0][0].shape[0] * sources[0][0].shape[4]
    done_cols = out_ref.shape[3] if out_ref is not None else 0
    shape = (steps, gap_cols)
    step_index = gap_step + lax.broadcasted_iota(jnp.int32, shape, 0)
    upper = step_index <= gap_col + lax.broadcasted_iota(jnp.int32, shape, 1)
    ret_terms = [(*sources[source], kind) for source, kind in ret_terms]
    less_terms = [(*sources[source], kind) for source, kind in less_terms]
    for index in range(block):

        def advanced(part):
            gap = gap_less_ref[part, index].astype(jnp.float32)
            gap = gap - gap_more_ref[part, index].astype(jnp.float32)
            return jnp.where(upper, gap, 0.0).astype(jnp.bfloat16)

        def product(left, *right):
            return jnp.dot(
                left, jnp.concatenate(right, axis=0), preferred_element_type=jnp.float32
            )

        left = complex_left(less_terms, index)
        if not ret_terms:
            value = product(left, advanced(0), advanced(1))
        elif gap_col == first_col:
            value = product(
                jnp.concatenate([left, complex_left(ret_terms, index)], axis=1),
                advanced(0),
                advanced(1),
                lesser_ref[0, index],
                lesser_ref[1, index],
            )
        else:
            value = product(
                complex_left(ret_terms, index), lesser_ref[0, index], lesser_ref[1, index]
            )
            skipped = gap_col - first_col
            value = jnp.concatenate(
                [
                    value[:, :skipped],
                    value[:, skipped:] + product(left, advanced(0), advanced(1)),
                ],
                axis=1,
            )
        for part in range(2):
            one = value[part * rows : (part + 1) * rows]
            if has_total:
                one = total_ref[part, index] + one
            if out_ref is not None:
                out_ref[part, index] = (TIME_STEP * one[:, :done_cols]).astype(out_ref.dtype)
            if rest_ref is not None:
                rest_ref[part, index] = one[:, done_cols:]


def collide(order, sources, ret, less, functions, carried, cols, block, mixed=()):
    ret_terms, ret_step, ret_steps = ret
    less_terms, gap_step, gap_steps, gap_col = less
    less_all, more_all = functions
    first_col, last_col = cols
    total, output = carried
    _, local_k, _, col_count = less_all.shape
    rows = sources[0].shape[0] * sources[0].shape[4]
    span = col_count - first_col
    block = min(block, local_k)
    done_cols = last_col - first_col
    arrays, specs = ([], [])

    def take(array, shape, *place):
        arrays.append(array)
        specs.append(pl.BlockSpec(shape, lambda k, order: (0, k, *place)))

    for array in sources:
        count, kinds, _, _, sub_rows, width = array.shape
        arrays.append(array)
        specs.append(
            pl.BlockSpec(
                (count, kinds, 2, block, sub_rows, width), lambda k, order: (0, 0, 0, k, 0, 0)
            )
        )
    if ret_terms:
        take(less_all, (2, block, ret_steps, span), ret_step // ret_steps, first_col // span)
    gap_span = col_count - gap_col
    for array in (less_all, more_all):
        take(array, (2, block, gap_steps, gap_span), gap_step // gap_steps, gap_col // gap_span)
    if total is not None:
        take(total, (2, block, rows, span), 0, 0)
    out_specs, out_shape, aliases = ([], [], {})
    if done_cols:
        if output is not None:
            arrays.append(output)
            specs.append(pl.BlockSpec(memory_space=pl.ANY))
            aliases = {len(arrays): 0}
        out_specs.append(
            pl.BlockSpec(
                (2, block, rows, done_cols), lambda k, order: (0, k, 0, first_col // done_cols)
            )
        )
        out_shape.append(jax.ShapeDtypeStruct((2, local_k, rows, col_count), jnp.bfloat16))
    has_rest = last_col < col_count
    if has_rest:
        rest = col_count - last_col
        out_specs.append(pl.BlockSpec((2, block, rows, rest), lambda k, order: (0, k, 0, 0)))
        out_shape.append(jax.ShapeDtypeStruct((2, local_k, rows, rest), jnp.float32))
    plan = (
        len(sources),
        ret_terms,
        less_terms,
        first_col,
        gap_step,
        gap_col,
        total is not None,
        bool(aliases),
        has_rest,
        mixed,
    )
    work = ret_steps * span + gap_steps * gap_span
    results = list(
        pl.pallas_call(
            functools.partial(collide_kernel, plan),
            grid_spec=pltpu.PrefetchScalarGridSpec(
                num_scalar_prefetch=1, grid=(local_k // block,), in_specs=specs, out_specs=out_specs
            ),
            out_shape=out_shape,
            input_output_aliases=aliases,
            compiler_params=pltpu.CompilerParams(vmem_limit_bytes=VMEM_BYTES),
            cost_estimate=pl.CostEstimate(
                flops=8 * local_k * rows * work,
                bytes_accessed=12 * local_k * work + 8 * local_k * rows * span,
                transcendentals=0,
            ),
            name="collide",
        )(order, *arrays)
    )
    output = results.pop(0) if done_cols else None
    return (results.pop(0) if has_rest else None, output)


def on_device(lesser, greater, momentum_ids, window_start):
    _, local_k, row_count, col_count = lesser.shape
    groups, ranks = (lax.axis_size("mom"), lax.axis_size("trow"))
    group = lax.axis_index("mom")
    sub_rows = row_count // groups
    depth = 2 * local_k
    order = group ^ jnp.arange(groups, dtype=jnp.int32)
    far, near = (list(range(groups // 2, groups)), list(range(1, groups // 2)))
    offsets = [d for pair in zip(far, near + [0]) for d in pair if d]
    queues = {"far": (FAR_WINDOW, []), "near": (NEAR_WINDOW, []), "late": (LATE_WINDOW, [])}
    everyone = list(range(ranks))
    width = col_count // 4
    late_ranks = [r for r in everyone if (r + 1) * row_count > 3 * width]

    def send(make, arrays, offset, on_ranks):
        name = "far" if 2 * offset >= groups else "near"
        ahead, queue = queues["late" if on_ranks != everyone else name]
        if len(queue) >= ahead:
            arrays, _ = lax.optimization_barrier((arrays, queue[-ahead]))
        pairs = [(g * ranks + r, (g ^ offset) * ranks + r) for g in range(groups) for r in on_ranks]
        queue.append(lax.ppermute(make(*arrays), ("mom", "trow"), pairs))
        return queue[-1]

    def pack(offset, first, count, arrays):
        def rows_of(array):
            return lax.dynamic_slice(
                array,
                (0, 0, (group ^ offset) * sub_rows, first),
                (2, local_k, sub_rows, count),
            )

        both = jnp.stack([rows_of(array) for array in arrays])
        return both.transpose(3, 0, 1, 2, 4).reshape(1, sub_rows, 2, depth, count)

    def swap(array):
        return lax.all_to_all(array, "mom", split_axis=0, concat_axis=0, tiled=True)

    halves = [(0, 3 * width), (3 * width, width)]
    row_first = lax.axis_index("trow") * row_count + group * sub_rows
    row_times = row_first + jnp.arange(sub_rows, dtype=jnp.int32)
    first, count = halves[0]
    spread = {0: pack(0, first, count, (lesser, greater))}
    for d in offsets:
        spread[d] = send(
            lambda *arrays: pack(d, first, count, arrays), (lesser, greater), d, everyone
        )
    first, count = halves[1]
    both = jnp.stack([lesser[..., first:], greater[..., first:]])
    both = both.reshape(2, 2, local_k, groups, sub_rows, count).transpose(3, 4, 0, 1, 2, 5)
    both, _ = lax.optimization_barrier((both, [spread[d] for d in offsets]))
    both = swap(both.reshape(groups, sub_rows, 2, depth, count))
    spreads = [[spread[d] for d in range(groups)], both]

    functions = tuple(
        lax.all_gather(array, "trow", axis=2, tiled=True) for array in (lesser, greater)
    )
    forward, backward = transforms(
        momentum_ids.reshape(groups, local_k)[order].reshape(-1), groups
    )
    row_drive = drive(window_start, row_times)

    def born_part(part, before=None):
        first, count = halves[part]
        col_index = first + jnp.arange(count, dtype=jnp.int32)
        weight = row_drive[:, None] * drive(window_start, col_index)[None, :]
        mask = (row_times[:, None] >= col_index[None, :]).astype(jnp.float32)
        if before is not None:
            weight, _ = lax.optimization_barrier((weight, before))
        sigma = born(order, spreads[part], forward, backward, weight[:, None], mask[:, None])
        return with_layout_constraint(sigma.transpose(0, 1, 3, 2, 4), Layout((0, 1, 2, 3, 4)))

    def late_ret(sigma):
        got = {0: sigma[group][1:]}
        for d in [*far, *near]:
            got[d] = send(lambda array: array[group ^ d][1:], (sigma,), d, late_ranks)
        return in_order(jnp.stack([got[d] for d in range(groups)]), True)

    def in_order(got, mixed):
        kinds, count = (got.shape[1], got.shape[4])
        got = got.reshape(groups, kinds, 2, local_k, sub_rows, count)
        if sub_rows % 16 == 0:
            return got
        got = (got[order] if mixed else got).transpose(1, 2, 3, 0, 4, 5)
        return got.reshape(1, kinds, 2, local_k, groups * sub_rows, count)

    sigma, _ = lax.optimization_barrier((born_part(0), spreads[1]))
    low = in_order(swap(sigma), False)
    sigma = born_part(1)
    high_ret = late_ret(sigma)
    high, _ = lax.optimization_barrier((sigma[:, :1], (low, high_ret)))
    high = in_order(swap(high), False)
    carried = collide(
        order,
        [low, high_ret],
        ([(0, 1), (1, 0)], 0, col_count),
        ([(0, 0)], 0, 3 * width, 0),
        functions,
        (None, None),
        (0, 3 * width),
        2,
        () if sub_rows % 16 else (1,),
    )
    carried = collide(
        order,
        [high],
        ((), 0, 0),
        ([(0, 0)], 3 * width, width, 3 * width),
        functions,
        carried,
        (3 * width, col_count),
        8,
    )
    return carried[1]


def solution(mesh):
    return jax.shard_map(
        on_device,
        mesh=mesh,
        in_specs=(P(None, "mom", "trow", None), P(None, "mom", "trow", None), P(), P()),
        out_specs=P(None, "mom", "trow", None),
        check_vma=False,
    )
```
